128 devices in a mesh: lat: 16 (over z, y), fld: 8 (over x, core).
Axes of the slice: x: 4, y: 4, z: 4, core: 2. Of those that a mesh axis runs over, the one named last changes fastest.
Arguments:
- spectral: bfloat16 [640, 24, 2, 8, 1281], P('lat', 'fld'), may hold values from -0.25 to 0.25
- legendre: bfloat16 [640, 1281, 128], P('lat'), may hold values from -0.15625 to 0.15625
- pair_of_slot: int32 [640], replicated, may hold values from 0 to 639, each once
- quad_weights: float32 [128], P('lat'), may hold values from 1.5 to 8
- departure_row: int32 [24, 128, 3072], P(None, 'lat', 'fld'), may hold values from 1 to 125, as said below
- departure_column: int32 [24, 128, 3072], P(None, 'lat', 'fld'), may hold values from 0 to 3071, as said below
- fraction_row: float32 [24, 128, 3072], P(None, 'lat', 'fld'), may hold values from 0 to 1
- fraction_column: float32 [24, 128, 3072], P(None, 'lat', 'fld'), may hold values from 0 to 1
- regime: int32 [128, 3072], P('lat', 'fld'), may hold values from 0 to 15
- production: float32 [16, 8], replicated, may hold values from -3 to 3
- loss_rate: float32 [16, 8], replicated, may hold values from 0.05 to 3
Outputs:
- spectral_out: bfloat16 [640, 24, 2, 8, 1281], P('lat', 'fld')
- tracers_out: bfloat16 [24, 8, 128, 3072], P(None, None, 'lat', 'fld')
The draws below stay inside these ranges and needn't reach their ends.
Inputs may be any that keep to these rules, and one draw needn't show every extreme that they name: `pair_of_slot`: every pair appears in exactly one slot. `departure_row`: the arrival row plus an offset of -2 to 1, moved into the bounds. `departure_column`: the arrival column plus an offset of -2 to 1, modulo 3072.
All inputs are finite; a program needn't handle non-finite values.
Results may differ from the reference program's by a relative error of at most 0.014.
Values may be sent and summed in bfloat16 or wider, within the bound.
No kernel may reach another device: no remote copies, remote signals or barrier semaphores. Data moves between devices by JAX's collectives and lax.ppermute only.
A program may use at most 192 MiB of HBM per device.

```python
import math
import jax
import jax.numpy as jnp
from jax import lax

M = 1280
NLON = 3072
NTRC = 8
NTAB = 16
PAIRS = 640
KROW = 1281
LATW = 128
LEV = 24


def draw_departure_row(key, part):
    key = jax.random.fold_in(key, 11)
    arrival = lax.broadcasted_iota(jnp.int32, (LEV, LATW, NLON), 1)
    offset = jax.random.randint(key, (LEV, LATW, NLON), -2, 2)
    return jnp.clip(arrival + offset, 1, LATW - 3).astype(jnp.int32)


def draw_departure_column(key, part):
    key = jax.random.fold_in(key, 23)
    arrival = lax.broadcasted_iota(jnp.int32, (LEV, LATW, NLON), 2)
    offset = jax.random.randint(key, (LEV, LATW, NLON), -2, 2)
    return ((arrival + offset) % NLON).astype(jnp.int32)


def plant(result, key, least, high):
    dims = result.shape
    index_at = [jax.random.randint(jax.random.fold_in(key, axis), (), 0, dims[axis]) for axis in range(len(dims))]
    result = result.at[tuple(index_at)].set(least)
    longest = dims.index(max(dims))
    index_at[longest] = (index_at[longest] + 1) % dims[longest]
    return result.at[tuple(index_at)].set(high)


def block_scale(rng, dims, split, smallest, largest):
    level, own = 1.0, jax.random.fold_in(rng, 6)
    for axis_at, parts in split:
        draws = jnp.exp(jax.random.uniform(jax.random.fold_in(own, axis_at), (parts,), jnp.float32, smallest / len(split), largest / len(split)))
        level = level * jnp.repeat(draws, dims[axis_at] // parts).reshape([-1 if axis == axis_at else 1 for axis in range(len(dims))])
    return level


def centred(rng, shape, width, bound, cuts=(), kind=jnp.bfloat16):
    values = width * jax.random.normal(rng, shape, jnp.float32)
    if cuts:
        values = values * block_scale(rng, shape, cuts, -0.22, 0.18)
    return jnp.clip(values, -bound, bound).astype(kind)


def setup_inputs(seed: int = 0) -> dict:
    seeds = jax.random.split(jax.random.key(seed), 12)
    spectral = centred(seeds[0], (PAIRS, LEV, 2, NTRC, KROW), 0.04, 0.25, ((0, 16), (1, 8)))
    legendre = centred(seeds[1], (PAIRS, KROW, LATW), M ** -0.5, 0.15625, ((0, 16),))
    pair_of_slot = jax.random.permutation(seeds[2], PAIRS).astype(jnp.int32)
    quad_weights = jnp.clip(jnp.exp(math.log(8.0) - 1.6739764 * jax.random.uniform(seeds[3], (LATW,), jnp.float32) ** block_scale(seeds[3], (LATW,), ((0, 16),), -0.2, 0.2)), 1.5, 8.0)
    departure_row = draw_departure_row(jax.random.fold_in(seeds[11], 71), 0)
    departure_column = draw_departure_column(jax.random.fold_in(seeds[11], 71), 0)
    fraction_row = jnp.clip(1.0 * jax.random.uniform(seeds[6], (LEV, LATW, NLON), jnp.float32) ** block_scale(seeds[6], (LEV, LATW, NLON), ((1, 16), (2, 8)), -0.2, 0.2), 0.0, 1.0)
    fraction_column = jnp.clip(1.0 * jax.random.uniform(seeds[7], (LEV, LATW, NLON), jnp.float32) ** block_scale(seeds[7], (LEV, LATW, NLON), ((1, 16), (2, 8)), -0.2, 0.2), 0.0, 1.0)
    regime = plant(jax.random.randint(seeds[8], (LATW, NLON), 0, NTAB), jax.random.fold_in(seeds[8], 1), 0, NTAB - 1).astype(jnp.int32)
    production = centred(seeds[9], (NTAB, NTRC), 0.5, 3.0, (), jnp.float32)
    loss_rate = jnp.clip(jnp.exp(jax.random.uniform(seeds[10], (NTAB, NTRC), jnp.float32, math.log(0.05), math.log(3.0))), 0.05, 3.0)
    return {"spectral": spectral, "legendre": legendre, "pair_of_slot": pair_of_slot, "quad_weights": quad_weights, "departure_row": departure_row, "departure_column": departure_column, "fraction_row": fraction_row, "fraction_column": fraction_column, "regime": regime, "production": production, "loss_rate": loss_rate}


def cubic_weights(fraction):
    return (-fraction * (fraction - 1.0) * (fraction - 2.0) / 6.0, (fraction + 1.0) * (fraction - 1.0) * (fraction - 2.0) / 2.0, -(fraction + 1.0) * fraction * (fraction - 2.0) / 2.0, (fraction + 1.0) * fraction * (fraction - 1.0) / 6.0)

def reference(spectral, legendre, pair_of_slot, quad_weights, departure_row, departure_column, fraction_row, fraction_column, regime, production, loss_rate):
    block_size = math.gcd(PAIRS, 16)
    block_count = PAIRS // block_size
    row_index = lax.broadcasted_iota(jnp.int32, (PAIRS, KROW), 1)
    keep_mask = row_index < (M - pair_of_slot)[:, None]
    spec_blocks = spectral.reshape(block_count, block_size, LEV * 2 * NTRC, KROW)
    table_blocks = legendre.reshape(block_count, block_size, KROW, LATW)
    keep_blocks = keep_mask.reshape(block_count, block_size, KROW)

    def legendre_back(block_items):
        spec_part, table_part, keep_part = block_items
        packed = spec_part.astype(jnp.float32)
        side_mask = keep_part[:, None, :]
        zero_value = jnp.zeros((), jnp.float32)
        both_sides = jnp.concatenate([jnp.where(side_mask, packed, zero_value), jnp.where(side_mask, zero_value, packed)], axis=1)
        return jnp.einsum('pck,pkj->jpc', both_sides, table_part.astype(jnp.float32))
    partial_value = lax.map(legendre_back, (spec_blocks, table_blocks, keep_blocks))
    fourier_coeffs = jnp.transpose(partial_value, (1, 0, 2, 3)).reshape(LATW, PAIRS, 2, LEV, 2, NTRC)
    wave_numbers = jnp.stack([pair_of_slot, M - 1 - pair_of_slot], axis=1).reshape(-1).astype(jnp.int32)
    wave_scale = jnp.where(wave_numbers == 0, float(NLON), NLON / 2.0)
    real_part = jnp.transpose(fourier_coeffs[:, :, :, :, 0, :], (3, 4, 0, 1, 2)).reshape(LEV, NTRC, LATW, 2 * PAIRS)
    imag_part = jnp.transpose(fourier_coeffs[:, :, :, :, 1, :], (3, 4, 0, 1, 2)).reshape(LEV, NTRC, LATW, 2 * PAIRS)
    spectrum_values = lax.complex(real_part * wave_scale, imag_part * wave_scale)
    spectrum = jnp.zeros((LEV, NTRC, LATW, NLON // 2 + 1), spectrum_values.dtype).at[..., wave_numbers].set(spectrum_values)
    grid_values = jnp.fft.irfft(spectrum, n=NLON, axis=-1)
    flat_grid = grid_values.reshape(LEV, NTRC, LATW * NLON)
    weights_row = cubic_weights(fraction_row)
    weights_column = cubic_weights(fraction_column)
    advected = jnp.zeros(flat_grid.shape, flat_grid.dtype)
    for lat_step in range(4):
        for lon_step in range(4):
            gather_index = (departure_row + lat_step - 1) * NLON + (departure_column + lon_step - 1) % NLON
            gather_index = jnp.broadcast_to(gather_index.reshape(LEV, 1, LATW * NLON), flat_grid.shape)
            picked = jnp.take_along_axis(flat_grid, gather_index, axis=2)
            advected = advected + (weights_row[lat_step] * weights_column[lon_step]).reshape(LEV, 1, LATW * NLON) * picked
    supply = jnp.transpose(production[regime], (2, 0, 1)).reshape(1, NTRC, LATW * NLON)
    loss_values = jnp.transpose(loss_rate[regime], (2, 0, 1)).reshape(1, NTRC, LATW * NLON)
    chemistry = ((advected + supply) / (1.0 + loss_values)).reshape(LEV, NTRC, LATW, NLON)
    tracers_out = chemistry.astype(jnp.bfloat16)
    analysed_spectrum = jnp.fft.rfft(chemistry, axis=-1)
    chosen = analysed_spectrum[..., wave_numbers] * (1.0 / math.sqrt(NLON))
    stacked = jnp.stack([jnp.real(chosen), jnp.imag(chosen)], axis=-1).reshape(LEV, NTRC, LATW, PAIRS, 2, 2)
    analysed = jnp.transpose(stacked, (2, 3, 4, 0, 5, 1))
    weighted = (analysed * quad_weights[:, None, None, None, None, None]).astype(jnp.bfloat16)
    weighted = weighted.reshape(LATW, block_count, block_size, 4 * LEV * NTRC).transpose(1, 0, 2, 3)

    def legendre_forward(block_items):
        coeff_part, table_part, keep_part = block_items
        both_sides = jnp.einsum('jpc,pkj->pck', coeff_part.astype(jnp.float32), table_part.astype(jnp.float32))
        half_count = both_sides.shape[1] // 2
        return jnp.where(keep_part[:, None, :], both_sides[:, :half_count], both_sides[:, half_count:])
    merged = lax.map(legendre_forward, (weighted, table_blocks, keep_blocks))
    spectral_out = merged.reshape(PAIRS, LEV, 2, NTRC, KROW).astype(jnp.bfloat16)
    return (spectral_out, tracers_out)
```

```python
import functools
import math

import jax
import jax.numpy as jnp
import numpy as np
from jax import lax
from jax.experimental import pallas as pl
from jax.experimental.pallas import tpu as pltpu
from jax.sharding import PartitionSpec as P

M = 1280
NLON = 3072
F32 = jnp.float32
BF16 = jnp.bfloat16
ROW_ORDER = (0, 1, 2, 5, 6, 7, 3, 4)
VMEM_LIMIT = 50 * 1024 * 1024


def params():
    return pltpu.CompilerParams(vmem_limit_bytes=VMEM_LIMIT)


def tables(segments):
    wave = np.stack([np.arange(M // 2), M - 1 - np.arange(M // 2)])
    wave = np.repeat(wave[:, None], 2, axis=1).reshape(-1)
    part = np.tile(np.repeat([0, 1], M // 2), 2)
    circle = 2.0 * np.pi * np.arange(NLON) / NLON
    pair = np.stack([np.cos(circle), -np.sin(circle)]).astype(np.float32)
    width = NLON // segments
    first = np.arange(segments)[:, None] * width
    edge = np.concatenate([first + np.arange(-3, 0), first + width + np.arange(3)], axis=1)

    def rows(columns):
        phase = wave[:, None] * columns[None, :] % NLON
        return pair[part[:, None], phase]

    whole = rows(np.arange(NLON))
    sides = rows(edge.reshape(-1) % NLON).reshape(-1, segments, 6)
    sides = np.pad(sides, ((0, 0), (0, 0), (0, 2))).reshape(len(wave), -1).T
    return jnp.asarray(whole, BF16), jnp.asarray(sides, BF16)


def legendre_back(own_pairs, packed, legendre, count):
    pair_dev, rows, length = packed.shape
    lats = legendre.shape[2]
    group = 8
    steps = pair_dev // group
    lat_dev = lats // count

    def body(pairs, spec_ref, table_ref, out_ref, turned, wide):
        step = pl.program_id(0)
        for i in range(group):
            limit = M - pairs[step * group + i]
            keep = lax.broadcasted_iota(jnp.int32, (1, length), 1) < limit
            keep = jnp.where(keep, 1.0, 0.0).astype(BF16)
            values = spec_ref[i]
            low = values * keep
            both = jnp.concatenate([low, values - low], axis=0)
            result = jnp.dot(both, table_ref[i], preferred_element_type=F32)
            turned[i * lats : (i + 1) * lats, : 2 * rows] = result.T
        start = pl.multiple_of(step * group, group)
        for d in range(count):
            pieces = [
                turned[pl.ds(d * lat_dev + j, group, stride=lats), :][:, : 2 * rows]
                for j in range(lat_dev)
            ]
            wide[d, pl.ds(start, group), :] = jnp.concatenate(pieces, axis=1)

        @pl.when(step == steps - 1)
        def _():
            out_ref[...] = wide[...].astype(BF16)

    return pl.pallas_call(
        body,
        out_shape=jax.ShapeDtypeStruct((count, pair_dev, 2 * rows * lat_dev), BF16),
        grid=(steps,),
        in_specs=[
            pl.BlockSpec(memory_space=pltpu.SMEM),
            pl.BlockSpec((group, rows, length), lambda g: (g, 0, 0)),
            pl.BlockSpec((group, length, lats), lambda g: (g, 0, 0)),
        ],
        out_specs=pl.BlockSpec((count, pair_dev, 2 * rows * lat_dev), lambda g: (0, 0, 0)),
        scratch_shapes=[
            pltpu.VMEM((group * lats, 128), F32),
            pltpu.VMEM((count, pair_dev, 2 * rows * lat_dev), F32),
        ],
        compiler_params=params(),
        name="legendre_back",
    )(own_pairs, packed, legendre)


def one_hot(pair_row):
    count = pair_row.shape[1]
    hit = lax.broadcasted_iota(jnp.int32, (count, count), 0) == pair_row
    return jnp.where(hit, 1.0, 0.0).astype(BF16)


def fourier_back(pair_row, received, table, sides, lev_dev, tracers, lat_dev, segments):
    pairs = pair_row.shape[1]
    width = NLON // segments
    rows = lat_dev * lev_dev * tracers
    near = 3 * lev_dev * tracers

    def body(pair_ref, in_ref, table_ref, side_ref, out_ref, left, edges):
        step = pl.program_id(0)

        @pl.when(step == 0)
        def _():
            data = in_ref[...].astype(F32).reshape(pairs, -1).astype(BF16)
            natural = jnp.dot(one_hot(pair_ref[...]), data, preferred_element_type=F32).T
            for s in range(2):
                for r in range(2):
                    pieces = []
                    for j in ROW_ORDER:
                        for l in range(lev_dev):
                            at = (((j * 2 + s) * lev_dev + l) * 2 + r) * tracers
                            pieces.append(natural[at : at + tracers])
                    at = (2 * s + r) * pairs
                    left[:, at : at + pairs] = jnp.concatenate(pieces, axis=0).astype(BF16)
            edges[...] = jnp.zeros_like(edges)
            edges[:, :rows] = lax.dot_general(
                side_ref[...], left[...], (((1,), (1,)), ((), ())), preferred_element_type=F32
            )

        result = jnp.dot(left[...], table_ref[...], preferred_element_type=F32)
        edge = edges[pl.ds(pl.multiple_of(step * 8, 8), 8), :]
        out_ref[0, : near + 8, :] = jnp.concatenate([result[:near], edge], axis=0).astype(BF16)
        out_ref[0, near + 8 :, :] = result[near:].astype(BF16)

    return pl.pallas_call(
        body,
        out_shape=jax.ShapeDtypeStruct((segments, rows + 8, width), BF16),
        grid=(segments,),
        in_specs=[
            pl.BlockSpec((1, pairs), lambda q: (0, 0)),
            pl.BlockSpec(received.shape, lambda q: (0, 0, 0)),
            pl.BlockSpec((4 * pairs, width), lambda q: (0, q)),
            pl.BlockSpec(sides.shape, lambda q: (0, 0)),
        ],
        out_specs=pl.BlockSpec((1, rows + 8, width), lambda q: (q, 0, 0)),
        scratch_shapes=[
            pltpu.VMEM((rows, 4 * pairs), BF16),
            pltpu.VMEM((segments * 8, width), F32),
        ],
        compiler_params=params(),
        name="fourier_back",
    )(pair_row, received, table, sides)


def cubic_weights(fraction):
    less, more, far = fraction - 1.0, fraction + 1.0, fraction - 2.0
    inner, outer = fraction * less, more * far
    return (
        inner * far * (-1.0 / 6.0),
        outer * less * 0.5,
        outer * fraction * -0.5,
        inner * more * (1.0 / 6.0),
    )


def shift_weights(offset, fraction):
    weights = cubic_weights(fraction)
    at = [offset == step - 2 for step in range(4)]
    zero = jnp.zeros_like(fraction)
    result = []
    for shift in range(7):
        total = zero
        for step in range(4):
            if 0 <= shift - step < 4:
                total = jnp.where(at[step], weights[shift - step], total)
        result.append(total)
    return result


def advect(where, received, before, after, drow, dcol, frow, fcol, regime, production, loss_rate):
    segments, block_rows, width = received.shape
    levels, lat_dev, _ = drow.shape
    regimes, tracers = production.shape
    lev_dev = levels // segments
    step_rows = lev_dev * tracers
    side_rows = before.shape[1]
    own_rows = lat_dev * step_rows
    rows_all = lat_dev + 6
    blocks = width // 128

    def place(row):
        if row < 3:
            return side_rows - 3 * step_rows + row * step_rows, 0, (row + 3) * step_rows
        if row < 3 + lat_dev:
            spot = ROW_ORDER.index(row - 3)
            return side_rows + spot * step_rows + (8 if spot >= 3 else 0), 1, spot * step_rows
        spot = row - 3 - lat_dev
        return side_rows + block_rows + spot * step_rows, 2, spot * step_rows

    def body(
        where_ref, own_ref, before_ref, after_ref, drow_ref, dcol_ref, frow_ref, fcol_ref,
        regime_ref, production_ref, loss_ref, tracers_ref, send_ref,
        cells, edges, wide, shifted, row_w, col_w, supply, factor, turned, sent,
    ):
        step = pl.program_id(0)

        @pl.when(step == 0)
        def _():
            for j in range(lat_dev):
                now = regime_ref[j : j + 1, :]
                total = jnp.zeros((tracers, width), F32)
                loss = jnp.zeros((tracers, width), F32)
                for r in range(regimes):
                    hit = now == r
                    total = jnp.where(hit, production_ref[:, r : r + 1], total)
                    loss = jnp.where(hit, loss_ref[:, r : r + 1], loss)
                supply[j] = total
                factor[j] = 1.0 / (1.0 + loss)

        cells[:side_rows] = before_ref[0].astype(F32)
        cells[side_rows : side_rows + block_rows] = own_ref[0].astype(F32)
        cells[side_rows + block_rows :] = after_ref[0].astype(F32)
        starts = (0, side_rows + 3 * step_rows, side_rows + block_rows + 3 * step_rows)
        for k, start in enumerate(starts):
            tall = jnp.concatenate(
                [cells[start : start + 8, :256], jnp.zeros((120, 256), F32)], axis=0
            )
            edges[k] = tall.T

        arrival_row = lax.broadcasted_iota(jnp.int32, (lat_dev, width), 0) + where_ref[0]
        arrival_col = lax.broadcasted_iota(jnp.int32, (lat_dev, width), 1) + where_ref[1]
        @pl.loop(0, lev_dev)
        def _(i):
            row_offset = drow_ref[i] - arrival_row
            ahead = dcol_ref[i] - arrival_col
            ahead = jnp.where(ahead > NLON // 2, ahead - NLON, ahead)
            ahead = jnp.where(ahead < -(NLON // 2), ahead + NLON, ahead)
            for k, value in enumerate(shift_weights(row_offset, frow_ref[i])):
                row_w[k] = value
            for k, value in enumerate(shift_weights(ahead, fcol_ref[i])):
                col_w[k] = value
            for row in range(rows_all):
                start, source, edge_start = place(row)
                start = pl.multiple_of(start + i * tracers, tracers)
                edge_start = pl.multiple_of(edge_start + i * tracers, tracers)
                edge = pltpu.roll(edges[source, pl.ds(edge_start, tracers), :], 125, 1)
                wide[:, :128] = edge
                wide[:, 128 : 128 + width] = cells[pl.ds(start, tracers), :]
                wide[:, 128 + width :] = edge
                for k in range(7):
                    shifted[k, row] = wide[:, 125 + k : 125 + k + width]

            for j in range(lat_dev):
                for b in range(blocks):
                    lanes = slice(b * 128, (b + 1) * 128)
                    total = None
                    across = [
                        jnp.broadcast_to(col_w[k, j : j + 1, lanes], (tracers, 128))
                        for k in range(7)
                    ]
                    for r in range(7):
                        line = None
                        for k in range(7):
                            term = across[k] * shifted[k, j + r, :, lanes]
                            line = term if line is None else line + term
                        line = line * row_w[r, j : j + 1, lanes]
                        total = line if total is None else total + line
                    value = (total + supply[j, :, lanes]) * factor[j, :, lanes]
                    turned[b, pl.ds(j, tracers, stride=lat_dev), :] = value
                    at = pl.multiple_of(j * step_rows + i * tracers, tracers)
                    sent[pl.ds(at, tracers), lanes] = value

            for b in range(blocks):
                lanes = slice(b * 128, (b + 1) * 128)
                out = turned[b].reshape(tracers, lat_dev, 128)
                tracers_ref[i, :, :, lanes] = out.astype(BF16)

        send_ref[0] = sent[...].astype(BF16)

    level_block = pl.BlockSpec((lev_dev, lat_dev, width), lambda f: (f, 0, 0))

    def part(rows):
        return pl.BlockSpec((1, rows, width), lambda f: (f, 0, 0))

    def whole(shape):
        return pl.BlockSpec(shape, lambda f: (0,) * len(shape))

    return pl.pallas_call(
        body,
        out_shape=(
            jax.ShapeDtypeStruct((levels, tracers, lat_dev, width), BF16),
            jax.ShapeDtypeStruct((segments, own_rows, width), BF16),
        ),
        grid=(segments,),
        in_specs=[
            pl.BlockSpec(memory_space=pltpu.SMEM),
            part(block_rows), part(side_rows), part(side_rows),
            level_block, level_block, level_block, level_block,
            whole((lat_dev, width)), whole((tracers, regimes)), whole((tracers, regimes)),
        ],
        out_specs=(
            pl.BlockSpec((lev_dev, tracers, lat_dev, width), lambda f: (f, 0, 0, 0)),
            part(own_rows),
        ),
        scratch_shapes=[
            pltpu.VMEM((block_rows + 2 * side_rows, width), F32),
            pltpu.VMEM((3, 256, 128), F32),
            pltpu.VMEM((tracers, width + 256), F32),
            pltpu.VMEM((7, rows_all, tracers, width), F32),
            pltpu.VMEM((7, lat_dev, width), F32),
            pltpu.VMEM((7, lat_dev, width), F32),
            pltpu.VMEM((lat_dev, tracers, width), F32),
            pltpu.VMEM((lat_dev, tracers, width), F32),
            pltpu.VMEM((blocks, tracers * lat_dev, 128), F32),
            pltpu.VMEM((own_rows, width), F32),
        ],
        compiler_params=params(),
        name="advect",
    )(
        where, received, before, after, drow, dcol, frow, fcol,
        regime, production.T, loss_rate.T,
    )


def fourier_forward(pair_row, quad, received, table, lev_dev, tracers, lat_dev, count):
    pairs = pair_row.shape[1]
    segments, rows, width = received.shape
    step_rows = lev_dev * tracers

    def body(pair_ref, quad_ref, in_ref, table_ref, out_ref, hits, natural):
        step = pl.program_id(0)

        @pl.when(step == 0)
        def _():
            hits[...] = one_hot(pair_ref[...])

        data = jnp.concatenate([in_ref[q] for q in range(segments)], axis=1)
        result = lax.dot_general(
            data, table_ref[...], (((1,), (1,)), ((), ())), preferred_element_type=F32
        )
        pieces = [
            result[j * step_rows : (j + 1) * step_rows] * quad_ref[j] for j in range(lat_dev)
        ]
        result = jnp.concatenate(pieces, axis=0).astype(BF16)
        result = jnp.dot(result, hits[...], preferred_element_type=F32)
        side, part = step // 2, step % 2
        for j in range(lat_dev):
            for l in range(lev_dev):
                at = (((j * 2 + side) * lev_dev + l) * 2 + part) * tracers
                start = (j * lev_dev + l) * tracers
                natural[pl.ds(pl.multiple_of(at, tracers), tracers), :] = result[
                    start : start + tracers
                ]

        @pl.when(step == 3)
        def _():
            turned = natural[...].T
            each = pairs // count
            for d in range(count):
                out_ref[d] = turned[d * each : (d + 1) * each].astype(BF16)

    shape = (count, pairs // count, 4 * rows)
    return pl.pallas_call(
        body,
        out_shape=jax.ShapeDtypeStruct(shape, BF16),
        grid=(4,),
        in_specs=[
            pl.BlockSpec((1, pairs), lambda g: (0, 0)),
            pl.BlockSpec(memory_space=pltpu.SMEM),
            pl.BlockSpec(received.shape, lambda g: (0, 0, 0)),
            pl.BlockSpec((pairs, NLON), lambda g: (g, 0)),
        ],
        out_specs=pl.BlockSpec(shape, lambda g: (0, 0, 0)),
        scratch_shapes=[pltpu.VMEM((pairs, pairs), BF16), pltpu.VMEM((4 * rows, pairs), F32)],
        compiler_params=params(),
        name="fourier_forward",
    )(pair_row, quad, received, table)


def legendre_forward(own_pairs, received, legendre):
    count, pair_dev, width = received.shape
    length, lats = legendre.shape[1:]
    lat_dev = lats // count
    rows = width // lat_dev
    group = 8

    def body(pairs, in_ref, table_ref, out_ref, turned):
        step = pl.program_id(0)

        @pl.when(step == 0)
        def _():
            for s in range(count):
                values = in_ref[s].astype(F32)
                for j in range(lat_dev):
                    piece = values[:, j * rows : (j + 1) * rows]
                    piece = jnp.concatenate(
                        [piece, jnp.zeros((pair_dev, 128 - rows), F32)], axis=1
                    )
                    turned[pl.ds(s * lat_dev + j, pair_dev, stride=lats), :] = piece

        for i in range(group):
            pair = step * group + i
            limit = M - pairs[pair]
            keep = lax.broadcasted_iota(jnp.int32, (1, length), 1) < limit
            left = turned[pl.ds(pl.multiple_of(pair * lats, lats), lats), :].T[:rows]
            both = lax.dot_general(
                left.astype(BF16),
                table_ref[i],
                (((1,), (1,)), ((), ())),
                preferred_element_type=F32,
            )
            out_ref[i] = jnp.where(keep, both[: rows // 2], both[rows // 2 :]).astype(BF16)

    return pl.pallas_call(
        body,
        out_shape=jax.ShapeDtypeStruct((pair_dev, rows // 2, length), BF16),
        grid=(pair_dev // group,),
        in_specs=[
            pl.BlockSpec(memory_space=pltpu.SMEM),
            pl.BlockSpec(received.shape, lambda g: (0, 0, 0)),
            pl.BlockSpec((group, length, lats), lambda g: (g, 0, 0)),
        ],
        out_specs=pl.BlockSpec((group, rows // 2, length), lambda g: (g, 0, 0)),
        scratch_shapes=[pltpu.VMEM((pair_dev * lats, 128), F32)],
        compiler_params=params(),
        name="legendre_forward",
    )(own_pairs, received, legendre)


def per_device(
    spectral,
    legendre,
    pair_of_slot,
    quad_weights,
    departure_row,
    departure_column,
    fraction_row,
    fraction_column,
    regime,
    production,
    loss_rate,
):
    pair_dev, lev_dev, _, tracers, length = spectral.shape
    lat_dev, width = departure_row.shape[1:]
    count, segments = lax.axis_size("lat"), lax.axis_size("fld")
    band, segment = lax.axis_index("lat"), lax.axis_index("fld")
    table, sides = tables(segments)
    own_pairs = lax.dynamic_slice_in_dim(pair_of_slot, band * pair_dev, pair_dev)
    pair_row = pair_of_slot[None, :]
    exchange = functools.partial(lax.all_to_all, split_axis=0, concat_axis=0, tiled=True)

    packed = spectral.reshape(pair_dev, lev_dev * 2 * tracers, length)
    coeffs = legendre_back(own_pairs, packed, legendre, count)
    coeffs = exchange(coeffs, "lat")
    grid = fourier_back(pair_row, coeffs, table, sides, lev_dev, tracers, lat_dev, segments)
    grid = exchange(grid, "fld")
    near = 3 * lev_dev * tracers + 8
    up = [(i, (i + 1) % count) for i in range(count)]
    down = [(b, a) for a, b in up]
    before = lax.ppermute(grid[:, near - 8 : 2 * near - 8], "lat", up)
    after = lax.ppermute(grid[:, :near], "lat", down)
    where = jnp.stack([band * lat_dev, segment * width]).astype(jnp.int32)
    tracers_out, rows = advect(
        where, grid, before, after, departure_row, departure_column,
        fraction_row, fraction_column, regime, production, loss_rate,
    )
    rows = exchange(rows, "fld")
    quad = quad_weights * (1.0 / math.sqrt(NLON))
    back = fourier_forward(pair_row, quad, rows, table, lev_dev, tracers, lat_dev, count)
    back = exchange(back, "lat")
    spectral_out = legendre_forward(own_pairs, back, legendre)
    return spectral_out.reshape(spectral.shape), tracers_out


def solution(mesh):
    placed = (
        P("lat", "fld", None, None, None),
        P("lat", None, None),
        P(),
        P("lat"),
        P(None, "lat", "fld"),
        P(None, "lat", "fld"),
        P(None, "lat", "fld"),
        P(None, "lat", "fld"),
        P("lat", "fld"),
        P(),
        P(),
    )
    return jax.shard_map(
        per_device,
        mesh=mesh,
        in_specs=placed,
        out_specs=(P("lat", "fld", None, None, None), P(None, None, "lat", "fld")),
        check_vma=False,
    )
```

```python
import functools
import math

import jax
import jax.numpy as jnp
import numpy as np
from jax import lax
from jax.experimental import pallas as pl
from jax.experimental.pallas import tpu as pltpu
from jax.sharding import PartitionSpec as P

M = 1280
NLON = 3072
F32 = jnp.float32
BF16 = jnp.bfloat16
ROW_ORDER = (0, 1, 2, 5, 6, 7, 3, 4)
VMEM_LIMIT = 50 * 1024 * 1024


CHUNKS = ((0, 3),)


def params():
    return pltpu.CompilerParams(vmem_limit_bytes=VMEM_LIMIT)


def cost(us):
    return pl.CostEstimate(
        flops=int(us * 1e9), bytes_accessed=int(us * 2e6), transcendentals=0
    )


def row_groups(lev_dev, tracers):
    starts = []
    for first, levels in CHUNKS:
        for s in range(2):
            for l in range(first, first + levels):
                for r in range(2):
                    starts.append(((s * lev_dev + l) * 2 + r) * tracers)
    return starts


HALF = M // 4
QUARTER = NLON // 4
SPAN = QUARTER + 128


def pair_positions(pair):
    return (pair >> 1) + (pair & 1) * HALF


def tables(segments):
    spot = np.arange(HALF)
    wave = np.stack(
        [
            np.concatenate([2 * spot, M - 2 - 2 * spot]),
            np.concatenate([M - 1 - 2 * spot, 2 * spot + 1]),
        ]
    )
    wave = np.repeat(wave[:, None], 2, axis=1).reshape(-1)
    part = np.tile(np.repeat([0, 1], M // 2), 2)
    circle = 2.0 * np.pi * np.arange(NLON) / NLON
    pair = np.stack([np.cos(circle), -np.sin(circle)]).astype(np.float32)
    width = NLON // segments
    first = np.arange(segments)[:, None] * width
    edge = np.concatenate([first + np.arange(-3, 0), first + width + np.arange(3)], axis=1)

    def rows(columns):
        phase = wave[:, None] * columns[None, :] % NLON
        return pair[part[:, None], phase]

    quarter = rows(np.arange(SPAN))
    sides = rows(edge.reshape(-1) % NLON).reshape(-1, segments, 6)
    sides = np.pad(sides, ((0, 0), (0, 0), (0, 2))).reshape(len(wave), -1).T
    return jnp.asarray(quarter, BF16), jnp.asarray(sides, BF16)


def mirror():
    total = lax.broadcasted_iota(jnp.int32, (256, 128), 0) + lax.broadcasted_iota(
        jnp.int32, (256, 128), 1
    )
    return jnp.where(total == 128, 1.0, 0.0).astype(BF16)


def legendre_back(own_pairs, packed, legendre, count, lev_dev, tracers):
    pair_dev, rows, length = packed.shape
    lats = legendre.shape[2]
    depth = 256
    steps = (length - 1) // depth
    lat_dev = lats // count
    groups = row_groups(lev_dev, tracers)
    widths = [4 * levels * tracers for _, levels in CHUNKS]

    def body(pairs, spec_ref, spec_last, table_ref, table_last, *rest):
        outs, (sums, tall, turned) = rest[: len(CHUNKS)], rest[len(CHUNKS) :]
        step = pl.program_id(0)

        @pl.when(step == 0)
        def _():
            for p in range(pair_dev):
                column = spec_last[p][:, :1].astype(F32)
                row = table_last[0][p : p + 1, :].astype(F32)
                sums[p, :rows] = jnp.zeros((rows, lats), F32)
                sums[p, rows:] = column * row

        for k in range(0, depth, 8):
            piece = table_ref[k : k + 8].astype(F32)
            tall[k * pair_dev : (k + 8) * pair_dev] = piece.reshape(8 * pair_dev, lats)
        for p in range(pair_dev):
            limit = M - pairs[p] - step * depth
            keep = lax.broadcasted_iota(jnp.int32, (1, depth), 1) < limit
            keep = jnp.where(keep, 1.0, 0.0).astype(BF16)
            values = spec_ref[p]
            low = values * keep
            both = jnp.concatenate([low, values - low], axis=0)
            table = tall[pl.ds(p, depth, stride=pair_dev), :].astype(BF16)
            sums[p] += jnp.dot(both, table, preferred_element_type=F32)

        @pl.when(step == steps - 1)
        def _():
            for p in range(pair_dev):
                result = jnp.concatenate([sums[p, g : g + tracers] for g in groups], axis=0)
                turned[p * lats : (p + 1) * lats, : 2 * rows] = result.T
            for d in range(count):
                pieces = [
                    turned[pl.ds(d * lat_dev + j, pair_dev, stride=lats), :]
                    for j in range(lat_dev)
                ]
                first = 0
                for out, width in zip(outs, widths):
                    part = [piece[:, first : first + width] for piece in pieces]
                    out[d] = jnp.concatenate(part, axis=1).astype(BF16)
                    first += width

    return pl.pallas_call(
        body,
        out_shape=[
            jax.ShapeDtypeStruct((count, pair_dev, lat_dev * width), BF16) for width in widths
        ],
        grid=(steps,),
        in_specs=[
            pl.BlockSpec(memory_space=pltpu.SMEM),
            pl.BlockSpec((pair_dev, rows, depth), lambda g: (0, 0, g)),
            pl.BlockSpec((pair_dev, rows, 128), lambda g: (0, 0, steps * depth // 128)),
            pl.BlockSpec((depth, pair_dev, lats), lambda g: (g, 0, 0)),
            pl.BlockSpec((1, pair_dev, lats), lambda g: (steps * depth, 0, 0)),
        ],
        out_specs=[
            pl.BlockSpec((count, pair_dev, lat_dev * width), lambda g: (0, 0, 0))
            for width in widths
        ],
        scratch_shapes=[
            pltpu.VMEM((pair_dev, 2 * rows, lats), F32),
            pltpu.VMEM((depth * pair_dev, lats), F32),
            pltpu.VMEM((pair_dev * lats, 128), F32),
        ],
        compiler_params=params(),
        cost_estimate=cost(10),
        name="legendre_back",
    )(own_pairs, packed, packed, legendre, legendre)


def one_hot(pair_row):
    count = pair_row.shape[1]
    hit = lax.broadcasted_iota(jnp.int32, (count, count), 0) == pair_positions(pair_row)
    return jnp.where(hit, 1.0, 0.0).astype(BF16)


def fourier_back(pair_row, received, table, sides, lev_dev, tracers, lat_dev, segments):
    pairs = pair_row.shape[1]
    width = NLON // segments
    rows = lat_dev * lev_dev * tracers
    near = 3 * lev_dev * tracers
    blocks = width // 128

    def body(pair_ref, in_ref, table_hbm, side_ref, out_ref, left, table_ref, edges, sem):
        copy = pltpu.make_async_copy(table_hbm, table_ref, sem)
        copy.start()
        data = in_ref[...].astype(F32).reshape(pairs, -1).astype(BF16)
        natural = jnp.dot(one_hot(pair_ref[...]), data, preferred_element_type=F32).T
        first = lax.broadcasted_iota(jnp.int32, (1, pairs), 1) < HALF
        for r in range(2):
            by_side = []
            for s in range(2):
                pieces = []
                for j in ROW_ORDER:
                    for l in range(lev_dev):
                        at = (((j * 2 + s) * lev_dev + l) * 2 + r) * tracers
                        pieces.append(natural[at : at + tracers])
                by_side.append(jnp.concatenate(pieces, axis=0))
            for b in range(2):
                at = (2 * b + r) * pairs
                value = jnp.where(first, by_side[b], by_side[1 - b])
                left[:, at : at + pairs] = value.astype(BF16)
        edges[...] = jnp.zeros_like(edges)
        edges[:, :rows] = lax.dot_general(
            side_ref[...], left[...], (((1,), (1,)), ((), ())), preferred_element_type=F32
        )
        copy.wait()

        def product(k):
            at = slice(k * pairs, (k + 1) * pairs)
            return jnp.dot(left[:, at], table_ref[at, :], preferred_element_type=F32)

        cos_even, sin_even, cos_odd, sin_odd = (product(k) for k in range(4))
        both, differ = cos_even + cos_odd, cos_even - cos_odd
        both_sin, differ_sin = sin_even + sin_odd, sin_even - sin_odd
        ahead = (both + both_sin, differ + differ_sin)
        behind = ((differ - differ_sin).astype(BF16), (both - both_sin).astype(BF16))
        turn = mirror()

        def put(q, values):
            edge = edges[q * 8 : q * 8 + 8, :]
            top = jnp.concatenate([values[:near], edge], axis=0)
            out_ref[q, : near + 8, :] = top.astype(BF16)
            out_ref[q, near + 8 :, :] = values[near:].astype(BF16)

        for half in range(2):
            for q in range(2):
                put(4 * half + q, ahead[half][:, q * width : (q + 1) * width])
                pieces = []
                for k in range(blocks):
                    low = QUARTER - q * width - (k + 1) * 128
                    source = behind[half][:, low : low + 256]
                    pieces.append(jnp.dot(source, turn, preferred_element_type=F32))
                put(4 * half + 2 + q, jnp.concatenate(pieces, axis=1))

    return pl.pallas_call(
        body,
        out_shape=jax.ShapeDtypeStruct((segments, rows + 8, width), BF16),
        in_specs=[
            pl.BlockSpec(memory_space=pltpu.VMEM),
            pl.BlockSpec(memory_space=pltpu.VMEM),
            pl.BlockSpec(memory_space=pl.ANY),
            pl.BlockSpec(memory_space=pltpu.VMEM),
        ],
        out_specs=pl.BlockSpec(memory_space=pltpu.VMEM),
        scratch_shapes=[
            pltpu.VMEM((rows, 4 * pairs), BF16),
            pltpu.VMEM(table.shape, BF16),
            pltpu.VMEM((segments * 8, width), F32),
            pltpu.SemaphoreType.DMA,
        ],
        compiler_params=params(),
        cost_estimate=cost(5),
        name="fourier_back",
    )(pair_row, received, table, sides)


def cubic_weights(fraction):
    less, more, far = fraction - 1.0, fraction + 1.0, fraction - 2.0
    inner, outer = fraction * less, more * far
    return (
        inner * far * (-1.0 / 6.0),
        outer * less * 0.5,
        outer * fraction * -0.5,
        inner * more * (1.0 / 6.0),
    )


def shift_weights(offset, fraction):
    weights = cubic_weights(fraction)
    at = [offset == step - 2 for step in range(4)]
    zero = jnp.zeros_like(fraction)
    result = []
    for shift in range(7):
        total = zero
        for step in range(4):
            if 0 <= shift - step < 4:
                total = jnp.where(at[step], weights[shift - step], total)
        result.append(total)
    return result


def advect(
    where, received, before, after, drow, dcol, frow, fcol, regime, production, loss_rate,
    first, lev_dev, out,
):
    segments, block_rows, width = received.shape
    levels, lat_dev, _ = drow.shape
    regimes, tracers = production.shape
    lev_all = levels // segments
    step_rows = lev_dev * tracers
    side_rows = before.shape[1]
    own_rows = lat_dev * step_rows
    rows_all = lat_dev + 6
    blocks = width // 128

    def place(row):
        if row < 3:
            return side_rows - 3 * step_rows + row * step_rows, 0, (row + 3) * step_rows
        if row < 3 + lat_dev:
            spot = ROW_ORDER.index(row - 3)
            return side_rows + spot * step_rows + (8 if spot >= 3 else 0), 1, spot * step_rows
        spot = row - 3 - lat_dev
        return side_rows + block_rows + spot * step_rows, 2, spot * step_rows

    def body(
        where_ref, own_ref, before_ref, after_ref, drow_ref, dcol_ref, frow_ref, fcol_ref,
        regime_ref, production_ref, loss_ref, *rest,
    ):
        (
            tracers_ref, send_ref,
            cells, edges, wide, shifted, row_w, col_w, supply, factor, turned, sent,
        ) = rest[0 if out is None else 1 :]
        step = pl.program_id(0)

        @pl.when(step == 0)
        def _():
            for j in range(lat_dev):
                now = regime_ref[j : j + 1, :]
                total = jnp.zeros((tracers, width), F32)
                loss = jnp.zeros((tracers, width), F32)
                for r in range(regimes):
                    hit = now == r
                    total = jnp.where(hit, production_ref[:, r : r + 1], total)
                    loss = jnp.where(hit, loss_ref[:, r : r + 1], loss)
                supply[j] = total
                factor[j] = 1.0 / (1.0 + loss)

        cells[:side_rows] = before_ref[0].astype(F32)
        cells[side_rows : side_rows + block_rows] = own_ref[0].astype(F32)
        cells[side_rows + block_rows :] = after_ref[0].astype(F32)
        starts = (0, side_rows + 3 * step_rows, side_rows + block_rows + 3 * step_rows)
        for k, start in enumerate(starts):
            tall = jnp.concatenate(
                [cells[start : start + 8, :256], jnp.zeros((120, 256), F32)], axis=0
            )
            edges[k] = tall.T

        arrival_row = lax.broadcasted_iota(jnp.int32, (lat_dev, width), 0) + where_ref[0]
        arrival_col = lax.broadcasted_iota(jnp.int32, (lat_dev, width), 1) + where_ref[1]
        @pl.loop(0, lev_dev)
        def _(i):
            row_offset = drow_ref[0, first + i] - arrival_row
            ahead = dcol_ref[0, first + i] - arrival_col
            ahead = jnp.where(ahead > NLON // 2, ahead - NLON, ahead)
            ahead = jnp.where(ahead < -(NLON // 2), ahead + NLON, ahead)
            for k, value in enumerate(shift_weights(row_offset, frow_ref[0, first + i])):
                row_w[k] = value
            for k, value in enumerate(shift_weights(ahead, fcol_ref[0, first + i])):
                col_w[k] = value
            for row in range(rows_all):
                start, source, edge_start = place(row)
                start = pl.multiple_of(start + i * tracers, tracers)
                edge_start = pl.multiple_of(edge_start + i * tracers, tracers)
                edge = pltpu.roll(edges[source, pl.ds(edge_start, tracers), :], 125, 1)
                wide[row, :, :128] = edge
                wide[row, :, 128 : 128 + width] = cells[pl.ds(start, tracers), :]
                wide[row, :, 128 + width :] = edge
            for row in range(rows_all):
                for k in range(7):
                    shifted[k, row] = wide[row, :, 125 + k : 125 + k + width]

            for b in range(blocks):
                lanes = slice(b * 128, (b + 1) * 128)
                for top in range(0, lat_dev, 4):
                    across = [
                        [
                            jnp.broadcast_to(col_w[k, j : j + 1, lanes], (tracers, 128))
                            for k in range(7)
                        ]
                        for j in range(top, top + 4)
                    ]
                    totals = [None] * 4
                    for row in range(top, top + 10):
                        cell = [shifted[k, row, :, lanes] for k in range(7)]
                        for n in range(4):
                            r = row - top - n
                            if not 0 <= r < 7:
                                continue
                            line = across[n][0] * cell[0]
                            for k in range(1, 7):
                                line = line + across[n][k] * cell[k]
                            line = line * row_w[r, top + n : top + n + 1, lanes]
                            totals[n] = line if totals[n] is None else totals[n] + line
                    for n in range(4):
                        j = top + n
                        value = (totals[n] + supply[j, :, lanes]) * factor[j, :, lanes]
                        turned[b, pl.ds(j, tracers, stride=lat_dev), :] = value
                        at = pl.multiple_of(j * step_rows + i * tracers, tracers)
                        sent[pl.ds(at, tracers), lanes] = value

            for b in range(blocks):
                lanes = slice(b * 128, (b + 1) * 128)
                result = turned[b].reshape(tracers, lat_dev, 128)
                tracers_ref[0, i, :, :, lanes] = result.astype(BF16)

        send_ref[0] = sent[...].astype(BF16)

    level_block = pl.BlockSpec((1, lev_all, lat_dev, width), lambda f: (f, 0, 0, 0))

    def part(rows):
        return pl.BlockSpec((1, rows, width), lambda f: (f, 0, 0))

    def whole(shape):
        return pl.BlockSpec(shape, lambda f: (0,) * len(shape))

    def by_segment(array):
        return array.reshape(segments, lev_all, *array.shape[1:])

    operands = [
        where, received, before, after, *map(by_segment, (drow, dcol, frow, fcol)),
        regime, production.T, loss_rate.T,
    ]
    in_specs = [
        pl.BlockSpec(memory_space=pltpu.SMEM),
        part(block_rows), part(side_rows), part(side_rows),
        level_block, level_block, level_block, level_block,
        whole((lat_dev, width)), whole((tracers, regimes)), whole((tracers, regimes)),
    ]
    aliases = {}
    if out is not None:
        aliases = {len(operands): 0}
        operands.append(out)
        in_specs.append(pl.BlockSpec(memory_space=pl.ANY))
    assert first % lev_dev == 0
    return pl.pallas_call(
        body,
        out_shape=(
            jax.ShapeDtypeStruct((segments, lev_all, tracers, lat_dev, width), BF16),
            jax.ShapeDtypeStruct((segments, own_rows, width), BF16),
        ),
        grid=(segments,),
        in_specs=in_specs,
        out_specs=(
            pl.BlockSpec(
                (1, lev_dev, tracers, lat_dev, width), lambda f: (f, first // lev_dev, 0, 0, 0)
            ),
            part(own_rows),
        ),
        scratch_shapes=[
            pltpu.VMEM((block_rows + 2 * side_rows, width), F32),
            pltpu.VMEM((3, 256, 128), F32),
            pltpu.VMEM((rows_all, tracers, width + 256), F32),
            pltpu.VMEM((7, rows_all, tracers, width), F32),
            pltpu.VMEM((7, lat_dev, width), F32),
            pltpu.VMEM((7, lat_dev, width), F32),
            pltpu.VMEM((lat_dev, tracers, width), F32),
            pltpu.VMEM((lat_dev, tracers, width), F32),
            pltpu.VMEM((blocks, tracers * lat_dev, 128), F32),
            pltpu.VMEM((own_rows, width), F32),
        ],
        input_output_aliases=aliases,
        compiler_params=params(),
        cost_estimate=cost(7 * lev_dev),
        name="advect",
    )(*operands)


def fourier_forward(pair_row, quad, received, table, lev_dev, tracers, lat_dev, count):
    pairs = pair_row.shape[1]
    segments, rows, width = received.shape
    step_rows = lev_dev * tracers
    blocks = width // 128

    def body(pair_ref, quad_ref, in_ref, table_hbm, out_ref, table_ref, folded, sem):
        copy = pltpu.make_async_copy(table_hbm, table_ref, sem)
        copy.start()
        turn = mirror()
        zero = jnp.zeros((rows, 128), F32)

        def block(k):
            at = k % blocks * 128
            return in_ref[k // blocks, :, at : at + 128]

        def mirrored(i, end):
            low, high = end // 128 - i - 1, end // 128 - i
            if i == 0:
                return jnp.dot(block(low), turn[:128], preferred_element_type=F32)
            if i == QUARTER // 128:
                return jnp.dot(block(high), turn[128:], preferred_element_type=F32)
            both = jnp.concatenate([block(low), block(high)], axis=1)
            return jnp.dot(both, turn, preferred_element_type=F32)

        for i in range(SPAN // 128):
            inside = i < QUARTER // 128
            one = block(i).astype(F32) if inside else zero
            two = block(NLON // 256 + i).astype(F32) if inside else zero
            one_back, two_back = mirrored(i, NLON // 2), mirrored(i, NLON)
            outer, inner = one + two_back, one_back + two
            outer_less, inner_less = one - two_back, two - one_back
            lanes = slice(i * 128, (i + 1) * 128)
            folded[0, :, lanes] = (outer + inner).astype(BF16)
            folded[1, :, lanes] = (outer_less + inner_less).astype(BF16)
            folded[2, :, lanes] = (outer - inner).astype(BF16)
            folded[3, :, lanes] = (outer_less - inner_less).astype(BF16)
        hits = one_hot(pair_ref[...])
        copy.wait()

        def product(k):
            result = lax.dot_general(
                folded[k],
                table_ref[k * pairs : (k + 1) * pairs, :],
                (((1,), (1,)), ((), ())),
                preferred_element_type=F32,
            )
            pieces = [
                result[j * step_rows : (j + 1) * step_rows] * quad_ref[j] for j in range(lat_dev)
            ]
            return jnp.concatenate(pieces, axis=0)

        first = lax.broadcasted_iota(jnp.int32, (1, pairs), 1) < HALF
        groups = [None] * (4 * lat_dev * lev_dev)
        for r in range(2):
            by_parity = [product(r), product(2 + r)]
            for s in range(2):
                value = jnp.where(first, by_parity[s], by_parity[1 - s]).astype(BF16)
                value = jnp.dot(value, hits, preferred_element_type=F32)
                for j in range(lat_dev):
                    for l in range(lev_dev):
                        start = (j * lev_dev + l) * tracers
                        groups[((j * 2 + s) * lev_dev + l) * 2 + r] = value[
                            start : start + tracers
                        ]
        turned = jnp.concatenate(groups, axis=0).T
        each = pairs // count
        for d in range(count):
            out_ref[d] = turned[d * each : (d + 1) * each].astype(BF16)

    shape = (count, pairs // count, 4 * rows)
    return pl.pallas_call(
        body,
        out_shape=jax.ShapeDtypeStruct(shape, BF16),
        in_specs=[
            pl.BlockSpec(memory_space=pltpu.VMEM),
            pl.BlockSpec(memory_space=pltpu.SMEM),
            pl.BlockSpec(memory_space=pltpu.VMEM),
            pl.BlockSpec(memory_space=pl.ANY),
        ],
        out_specs=pl.BlockSpec(memory_space=pltpu.VMEM),
        scratch_shapes=[
            pltpu.VMEM(table.shape, BF16),
            pltpu.VMEM((4, rows, SPAN), BF16),
            pltpu.SemaphoreType.DMA,
        ],
        compiler_params=params(),
        cost_estimate=cost(5),
        name="fourier_forward",
    )(pair_row, quad, received, table)


def legendre_forward(own_pairs, received, legendre, lev_dev, tracers):
    count, pair_dev, _ = received[0].shape
    length, lats = legendre.shape[1:]
    lat_dev = lats // count
    widths = [4 * levels * tracers for _, levels in CHUNKS]
    rows = sum(widths)
    groups = row_groups(lev_dev, tracers)
    back = [groups.index(start) * tracers for start in range(0, rows, tracers)]
    group = 8

    def body(pairs, *rest):
        ins, (table_ref, out_ref, turned) = rest[: len(CHUNKS)], rest[len(CHUNKS) :]
        step = pl.program_id(0)

        @pl.when(step == 0)
        def _():
            for s in range(count):
                values = [ref[s].astype(F32) for ref in ins]
                for j in range(lat_dev):
                    piece = [v[:, j * w : (j + 1) * w] for v, w in zip(values, widths)]
                    piece.append(jnp.zeros((pair_dev, 128 - rows), F32))
                    piece = jnp.concatenate(piece, axis=1)
                    turned[pl.ds(s * lat_dev + j, pair_dev, stride=lats), :] = piece

        for i in range(group):
            pair = step * group + i
            limit = M - pairs[pair]
            keep = lax.broadcasted_iota(jnp.int32, (1, length), 1) < limit
            left = turned[pl.ds(pl.multiple_of(pair * lats, lats), lats), :].T
            left = jnp.concatenate([left[at : at + tracers] for at in back], axis=0)
            both = lax.dot_general(
                left.astype(BF16),
                table_ref[i],
                (((1,), (1,)), ((), ())),
                preferred_element_type=F32,
            )
            out_ref[i] = jnp.where(keep, both[: rows // 2], both[rows // 2 :]).astype(BF16)

    return pl.pallas_call(
        body,
        out_shape=jax.ShapeDtypeStruct((pair_dev, rows // 2, length), BF16),
        grid=(pair_dev // group,),
        in_specs=[
            pl.BlockSpec(memory_space=pltpu.SMEM),
            *[pl.BlockSpec(array.shape, lambda g: (0, 0, 0)) for array in received],
            pl.BlockSpec((group, length, lats), lambda g: (g, 0, 0)),
        ],
        out_specs=pl.BlockSpec((group, rows // 2, length), lambda g: (g, 0, 0)),
        scratch_shapes=[pltpu.VMEM((pair_dev * lats, 128), F32)],
        compiler_params=params(),
        cost_estimate=cost(13),
        name="legendre_forward",
    )(own_pairs, *received, legendre)


def per_device(
    spectral,
    legendre,
    pair_of_slot,
    quad_weights,
    departure_row,
    departure_column,
    fraction_row,
    fraction_column,
    regime,
    production,
    loss_rate,
):
    pair_dev, lev_dev, _, tracers, length = spectral.shape
    lat_dev, width = departure_row.shape[1:]
    count, segments = lax.axis_size("lat"), lax.axis_size("fld")
    band, segment = lax.axis_index("lat"), lax.axis_index("fld")
    table, sides = tables(segments)
    own_pairs = lax.dynamic_slice_in_dim(pair_of_slot, band * pair_dev, pair_dev)
    pair_row = pair_of_slot[None, :]
    exchange = functools.partial(lax.all_to_all, split_axis=0, concat_axis=0, tiled=True)

    packed = spectral.reshape(pair_dev, lev_dev * 2 * tracers, length)
    coeffs = legendre_back(
        own_pairs, packed, legendre.transpose(1, 0, 2), count, lev_dev, tracers
    )
    where = jnp.stack([band * lat_dev, segment * width]).astype(jnp.int32)
    quad = quad_weights * (1.0 / math.sqrt(NLON))
    up = [(i, (i + 1) % count) for i in range(count)]
    down = [(b, a) for a, b in up]
    back, tracers_out = [], None
    for (first, levels), part in zip(CHUNKS, coeffs):
        part = exchange(part, "lat")
        grid = fourier_back(pair_row, part, table, sides, levels, tracers, lat_dev, segments)
        grid = exchange(grid, "fld")
        near = 3 * levels * tracers + 8
        before = lax.ppermute(grid[:, near - 8 : 2 * near - 8], "lat", up)
        after = lax.ppermute(grid[:, :near], "lat", down)
        tracers_out, rows = advect(
            where, grid, before, after, departure_row, departure_column,
            fraction_row, fraction_column, regime, production, loss_rate,
            first, levels, tracers_out,
        )
        rows = exchange(rows, "fld")
        part = fourier_forward(pair_row, quad, rows, table, levels, tracers, lat_dev, count)
        back.append(exchange(part, "lat"))
    spectral_out = legendre_forward(own_pairs, back, legendre, lev_dev, tracers)
    tracers_out = tracers_out.reshape(-1, tracers, lat_dev, width)
    return spectral_out.reshape(spectral.shape), tracers_out


def solution(mesh):
    placed = (
        P("lat", "fld", None, None, None),
        P("lat", None, None),
        P(),
        P("lat"),
        P(None, "lat", "fld"),
        P(None, "lat", "fld"),
        P(None, "lat", "fld"),
        P(None, "lat", "fld"),
        P("lat", "fld"),
        P(),
        P(),
    )
    return jax.shard_map(
        per_device,
        mesh=mesh,
        in_specs=placed,
        out_specs=(P("lat", "fld", None, None, None), P(None, None, "lat", "fld")),
        check_vma=False,
    )
```

```python
import functools
import math

import jax
import jax.numpy as jnp
import numpy as np
from jax import lax
from jax.experimental import pallas as pl
from jax.experimental.pallas import tpu as pltpu
from jax.sharding import PartitionSpec as P

M = 1280
NLON = 3072
F32 = jnp.float32
BF16 = jnp.bfloat16
ROW_ORDER = (0, 1, 2, 5, 6, 7, 3, 4)
VMEM_LIMIT = 50 * 1024 * 1024


CHUNKS = ((0, 3),)


def params():
    return pltpu.CompilerParams(vmem_limit_bytes=VMEM_LIMIT)


def cost(us):
    return pl.CostEstimate(
        flops=int(us * 1e9), bytes_accessed=int(us * 2e6), transcendentals=0
    )


def row_groups(lev_dev, tracers):
    starts = []
    for first, levels in CHUNKS:
        for s in range(2):
            for l in range(first, first + levels):
                for r in range(2):
                    starts.append(((s * lev_dev + l) * 2 + r) * tracers)
    return starts


HALF = M // 4
QUARTER = NLON // 4
SPAN = QUARTER + 128


def pair_positions(pair):
    return (pair >> 1) + (pair & 1) * HALF


def tables(segments):
    spot = np.arange(HALF)
    wave = np.stack(
        [
            np.concatenate([2 * spot, M - 2 - 2 * spot]),
            np.concatenate([M - 1 - 2 * spot, 2 * spot + 1]),
        ]
    )
    wave = np.repeat(wave[:, None], 2, axis=1).reshape(-1)
    part = np.tile(np.repeat([0, 1], M // 2), 2)
    circle = 2.0 * np.pi * np.arange(NLON) / NLON
    pair = np.stack([np.cos(circle), -np.sin(circle)]).astype(np.float32)
    width = NLON // segments
    first = np.arange(segments)[:, None] * width
    edge = np.concatenate([first + np.arange(-3, 0), first + width + np.arange(3)], axis=1)

    def rows(columns):
        phase = wave[:, None] * columns[None, :] % NLON
        return pair[part[:, None], phase]

    quarter = rows(np.arange(SPAN))
    sides = rows(edge.reshape(-1) % NLON).reshape(-1, segments, 6)
    sides = np.pad(sides, ((0, 0), (0, 0), (0, 2))).reshape(len(wave), -1).T
    turned = quarter.reshape(4, -1, SPAN).transpose(0, 2, 1).reshape(-1, M // 2)
    return jnp.asarray(quarter, BF16), jnp.asarray(sides, BF16), jnp.asarray(turned, BF16)


def mirror():
    total = lax.broadcasted_iota(jnp.int32, (256, 128), 0) + lax.broadcasted_iota(
        jnp.int32, (256, 128), 1
    )
    return jnp.where(total == 128, 1.0, 0.0).astype(BF16)


def legendre_back(own_pairs, packed, legendre, count, lev_dev, tracers):
    pair_dev, rows, length = packed.shape
    lats = legendre.shape[2]
    depth = 256
    steps = (length - 1) // depth
    lat_dev = lats // count
    groups = row_groups(lev_dev, tracers)
    widths = [4 * levels * tracers for _, levels in CHUNKS]

    def body(pairs, spec_hbm, spec_last, table_hbm, table_last, *rest):
        outs, rest = rest[: len(CHUNKS)], rest[len(CHUNKS) :]
        spec_ref, table_ref, sums, tall, turned, spec_sem, table_sem = rest
        copies = []
        for step in range(steps):
            at = pl.ds(step * depth, depth)
            copies.append(
                (
                    pltpu.make_async_copy(table_hbm.at[at], table_ref.at[at], table_sem.at[step]),
                    pltpu.make_async_copy(
                        spec_hbm.at[:, :, at], spec_ref.at[:, :, at], spec_sem.at[step]
                    ),
                )
            )
        for pair in copies:
            for copy in pair:
                copy.start()
        for p in range(pair_dev):
            column = spec_last[p][:, :1].astype(F32)
            row = table_last[0][p : p + 1, :].astype(F32)
            sums[p, :rows] = jnp.zeros((rows, lats), F32)
            sums[p, rows:] = column * row

        for step in range(steps):
            for copy in copies[step]:
                copy.wait()
            for k in range(0, depth, 8):
                at = step * depth + k
                piece = table_ref[at : at + 8].astype(F32)
                tall[k * pair_dev : (k + 8) * pair_dev] = piece.reshape(8 * pair_dev, lats)
            for p in range(pair_dev):
                limit = M - pairs[p] - step * depth
                keep = lax.broadcasted_iota(jnp.int32, (1, depth), 1) < limit
                keep = jnp.where(keep, 1.0, 0.0).astype(BF16)
                values = spec_ref[p, :, step * depth : (step + 1) * depth]
                low = values * keep
                both = jnp.concatenate([low, values - low], axis=0)
                table = tall[pl.ds(p, depth, stride=pair_dev), :].astype(BF16)
                sums[p] += jnp.dot(both, table, preferred_element_type=F32)

        for p in range(pair_dev):
            result = jnp.concatenate([sums[p, g : g + tracers] for g in groups], axis=0)
            turned[p * lats : (p + 1) * lats, : 2 * rows] = result.T
        for d in range(count):
            pieces = [
                turned[pl.ds(d * lat_dev + j, pair_dev, stride=lats), :]
                for j in range(lat_dev)
            ]
            first = 0
            for out, width in zip(outs, widths):
                part = [piece[:, first : first + width] for piece in pieces]
                out[d] = jnp.concatenate(part, axis=1).astype(BF16)
                first += width

    return pl.pallas_call(
        body,
        out_shape=[
            jax.ShapeDtypeStruct((count, pair_dev, lat_dev * width), BF16) for width in widths
        ],
        grid=(1,),
        in_specs=[
            pl.BlockSpec(memory_space=pltpu.SMEM),
            pl.BlockSpec(memory_space=pl.ANY),
            pl.BlockSpec((pair_dev, rows, 128), lambda g: (0, 0, steps * depth // 128)),
            pl.BlockSpec(memory_space=pl.ANY),
            pl.BlockSpec((1, pair_dev, lats), lambda g: (steps * depth, 0, 0)),
        ],
        out_specs=[
            pl.BlockSpec((count, pair_dev, lat_dev * width), lambda g: (0, 0, 0))
            for width in widths
        ],
        scratch_shapes=[
            pltpu.VMEM((pair_dev, rows, steps * depth), BF16),
            pltpu.VMEM((steps * depth, pair_dev, lats), BF16),
            pltpu.VMEM((pair_dev, 2 * rows, lats), F32),
            pltpu.VMEM((depth * pair_dev, lats), F32),
            pltpu.VMEM((pair_dev * lats, 128), F32),
            pltpu.SemaphoreType.DMA((steps,)),
            pltpu.SemaphoreType.DMA((steps,)),
        ],
        compiler_params=params(),
        cost_estimate=cost(10),
        name="legendre_back",
    )(own_pairs, packed, packed, legendre, legendre)


def one_hot(pair_row):
    count = pair_row.shape[1]
    hit = lax.broadcasted_iota(jnp.int32, (count, count), 0) == pair_positions(pair_row)
    return jnp.where(hit, 1.0, 0.0).astype(BF16)


def fourier_back(pair_row, received, table, sides, lev_dev, tracers, lat_dev, segments):
    pairs = pair_row.shape[1]
    width = NLON // segments
    rows = lat_dev * lev_dev * tracers
    near = 3 * lev_dev * tracers
    blocks = width // 128

    def body(pair_ref, in_ref, table_hbm, side_ref, out_ref, left, table_ref, edges, sem):
        copy = pltpu.make_async_copy(table_hbm, table_ref, sem)
        copy.start()
        data = in_ref[...].astype(F32).reshape(pairs, -1).astype(BF16)
        natural = jnp.dot(one_hot(pair_ref[...]), data, preferred_element_type=F32).T
        first = lax.broadcasted_iota(jnp.int32, (1, pairs), 1) < HALF
        for r in range(2):
            by_side = []
            for s in range(2):
                pieces = []
                for j in ROW_ORDER:
                    for l in range(lev_dev):
                        at = (((j * 2 + s) * lev_dev + l) * 2 + r) * tracers
                        pieces.append(natural[at : at + tracers])
                by_side.append(jnp.concatenate(pieces, axis=0))
            for b in range(2):
                at = (2 * b + r) * pairs
                value = jnp.where(first, by_side[b], by_side[1 - b])
                left[:, at : at + pairs] = value.astype(BF16)
        edges[...] = jnp.zeros_like(edges)
        edges[:, :rows] = lax.dot_general(
            side_ref[...], left[...], (((1,), (1,)), ((), ())), preferred_element_type=F32
        )
        copy.wait()

        def product(k):
            at = slice(k * pairs, (k + 1) * pairs)
            return jnp.dot(left[:, at], table_ref[at, :], preferred_element_type=F32)

        cos_even, sin_even, cos_odd, sin_odd = (product(k) for k in range(4))
        both, differ = cos_even + cos_odd, cos_even - cos_odd
        both_sin, differ_sin = sin_even + sin_odd, sin_even - sin_odd
        ahead = (both + both_sin, differ + differ_sin)
        behind = ((differ - differ_sin).astype(BF16), (both - both_sin).astype(BF16))
        turn = mirror()

        def put(q, values):
            edge = edges[q * 8 : q * 8 + 8, :]
            top = jnp.concatenate([values[:near], edge], axis=0)
            out_ref[q, : near + 8, :] = top.astype(BF16)
            out_ref[q, near + 8 :, :] = values[near:].astype(BF16)

        for half in range(2):
            for q in range(2):
                put(4 * half + q, ahead[half][:, q * width : (q + 1) * width])
                pieces = []
                for k in range(blocks):
                    low = QUARTER - q * width - (k + 1) * 128
                    source = behind[half][:, low : low + 256]
                    pieces.append(jnp.dot(source, turn, preferred_element_type=F32))
                put(4 * half + 2 + q, jnp.concatenate(pieces, axis=1))

    return pl.pallas_call(
        body,
        out_shape=jax.ShapeDtypeStruct((segments, rows + 8, width), BF16),
        in_specs=[
            pl.BlockSpec(memory_space=pltpu.VMEM),
            pl.BlockSpec(memory_space=pltpu.VMEM),
            pl.BlockSpec(memory_space=pl.ANY),
            pl.BlockSpec(memory_space=pltpu.VMEM),
        ],
        out_specs=pl.BlockSpec(memory_space=pltpu.VMEM),
        scratch_shapes=[
            pltpu.VMEM((rows, 4 * pairs), BF16),
            pltpu.VMEM(table.shape, BF16),
            pltpu.VMEM((segments * 8, width), F32),
            pltpu.SemaphoreType.DMA,
        ],
        compiler_params=params(),
        cost_estimate=cost(5),
        name="fourier_back",
    )(pair_row, received, table, sides)


def cubic_weights(fraction):
    less, more, far = fraction - 1.0, fraction + 1.0, fraction - 2.0
    inner, outer = fraction * less, more * far
    return (
        inner * far * (-1.0 / 6.0),
        outer * less * 0.5,
        outer * fraction * -0.5,
        inner * more * (1.0 / 6.0),
    )


def shift_weights(offset, fraction):
    weights = cubic_weights(fraction)
    at = [offset == step - 2 for step in range(4)]
    zero = jnp.zeros_like(fraction)
    result = []
    for shift in range(7):
        total = zero
        for step in range(4):
            if 0 <= shift - step < 4:
                total = jnp.where(at[step], weights[shift - step], total)
        result.append(total)
    return result


def advect(where, cells_in, departure, lev_dev, tracers, lat_dev, chemistry=None):
    segments, _, width = cells_in[0].shape
    step_rows = lev_dev * tracers
    own_rows = lat_dev * step_rows
    blocks = width // 128
    per_step = 2
    counts = [array.shape[1] for array in cells_in]
    starts = [sum(counts[:k]) for k in range(len(counts))]
    if chemistry is None:
        rows_in = list(range(3, 3 + lat_dev))
        edge_rows = [3 * step_rows]
    else:
        rows_in = [0, 1, 2, 3 + lat_dev, 4 + lat_dev, 5 + lat_dev]
        edge_rows = [0, 3 * step_rows]

    def place(row):
        if row < 3:
            return starts[0] + 8 + row * step_rows, 0, (row + 3) * step_rows
        if row < 3 + lat_dev:
            spot = ROW_ORDER.index(row - 3)
            return starts[0] + spot * step_rows + (8 if spot >= 3 else 0), 0, spot * step_rows
        spot = row - 3 - lat_dev
        return starts[1] + spot * step_rows, 1, spot * step_rows

    def body(where_ref, *rest):
        cells_refs, rest = rest[: len(cells_in)], rest[len(cells_in) :]
        if chemistry is None:
            drow_ref, dcol_ref, frow_ref, fcol_ref, sums_ref, row_ref, col_ref = rest[:7]
            cells, edges, wide, shifted, row_w = rest[7:]
        else:
            sums_ref, row_ref, col_ref, regime_ref, production_ref, loss_ref = rest[:6]
            tracers_ref, send_ref, cells, edges, wide, shifted = rest[6:12]
            supply, factor, turned, sent = rest[12:]

            @pl.when(pl.program_id(0) == 0)
            def _():
                for j in range(lat_dev):
                    now = regime_ref[j : j + 1, :]
                    total = jnp.zeros((tracers, width), F32)
                    loss = jnp.zeros((tracers, width), F32)
                    for r in range(production_ref.shape[1]):
                        hit = now == r
                        total = jnp.where(hit, production_ref[:, r : r + 1], total)
                        loss = jnp.where(hit, loss_ref[:, r : r + 1], loss)
                    supply[j] = total
                    factor[j] = 1.0 / (1.0 + loss)

        def weigh(f, i):
            arrival_row = lax.broadcasted_iota(jnp.int32, (lat_dev, width), 0) + where_ref[0]
            arrival_col = lax.broadcasted_iota(jnp.int32, (lat_dev, width), 1) + where_ref[1]
            row_offset = drow_ref[f, i] - arrival_row
            ahead = dcol_ref[f, i] - arrival_col
            ahead = jnp.where(ahead > NLON // 2, ahead - NLON, ahead)
            ahead = jnp.where(ahead < -(NLON // 2), ahead + NLON, ahead)
            for k, value in enumerate(shift_weights(row_offset, frow_ref[f, i])):
                row_w[i, k] = value
            for k, value in enumerate(shift_weights(ahead, fcol_ref[f, i])):
                col_ref[f, i, k] = value
            for j in range(lat_dev):
                for at in range(3):
                    r = at - j if j < 3 else 3 + lat_dev + at - j
                    if 0 <= r < 7 and (j < 3 or j >= lat_dev - 3):
                        row_ref[f, i, at, j : j + 1, :] = row_w[i, r, j : j + 1, :]

        @pl.loop(0, per_step)
        def _(f):
            for k, ref in enumerate(cells_refs):
                cells[starts[k] : starts[k] + counts[k]] = ref[f].astype(F32)
                at = starts[k] + edge_rows[k]
                tall = jnp.concatenate(
                    [cells[at : at + 8, :256], jnp.zeros((120, 256), F32)], axis=0
                )
                edges[k] = tall.T

            for i in range(lev_dev):
                if chemistry is None:
                    weigh(f, i)
                for at, row in enumerate(rows_in):
                    start, source, edge_start = place(row)
                    start, edge_start = start + i * tracers, edge_start + i * tracers
                    edge = pltpu.roll(edges[source, edge_start : edge_start + tracers, :], 125, 1)
                    wide[i, at, :, :128] = edge
                    wide[i, at, :, 128 : 128 + width] = cells[start : start + tracers, :]
                    wide[i, at, :, 128 + width :] = edge
            for i in range(lev_dev):
                for at in range(len(rows_in)):
                    for k in range(7):
                        shifted[i, k, at] = wide[i, at, :, 125 + k : 125 + k + width]

            for i in range(lev_dev):
                for b in range(blocks):
                    lanes = slice(b * 128, (b + 1) * 128)
                    for top in range(0, lat_dev, 4):
                        across = [
                            [
                                jnp.broadcast_to(
                                    col_ref[f, i, k, j : j + 1, lanes], (tracers, 128)
                                )
                                for k in range(7)
                            ]
                            for j in range(top, top + 4)
                        ]
                        totals = [None] * 4
                        if chemistry is not None:
                            totals = [sums_ref[f, i, top + n, :, lanes] for n in range(4)]
                        for at, row in enumerate(rows_in):
                            near = [n for n in range(4) if 0 <= row - top - n < 7]
                            if not near:
                                continue
                            cell = [shifted[i, k, at, :, lanes] for k in range(7)]
                            for n in near:
                                r = row - top - n
                                line = across[n][0] * cell[0]
                                for k in range(1, 7):
                                    line = line + across[n][k] * cell[k]
                                j = slice(top + n, top + n + 1)
                                if chemistry is None:
                                    line = line * row_w[i, r, j, lanes]
                                else:
                                    line = line * row_ref[f, i, at % 3, j, lanes]
                                totals[n] = line if totals[n] is None else totals[n] + line
                        for n in range(4):
                            j = top + n
                            if chemistry is None:
                                sums_ref[f, i, j, :, lanes] = totals[n]
                                continue
                            value = (totals[n] + supply[j, :, lanes]) * factor[j, :, lanes]
                            turned[i, b, pl.ds(j, tracers, stride=lat_dev), :] = value
                            at = j * step_rows + i * tracers
                            sent[at : at + tracers, lanes] = value

                if chemistry is not None:
                    for b in range(blocks):
                        lanes = slice(b * 128, (b + 1) * 128)
                        result = turned[i, b].reshape(tracers, lat_dev, 128)
                        tracers_ref[f, i, :, :, lanes] = result.astype(BF16)

            if chemistry is not None:
                send_ref[f] = sent[...].astype(BF16)

    def split(*shape):
        return pl.BlockSpec((per_step, *shape), lambda g: (g,) + (0,) * len(shape))

    def whole(shape):
        return pl.BlockSpec(shape, lambda g: (0,) * len(shape))

    lev_all = departure[0].shape[1]
    operands = [where, *cells_in, *departure]
    in_specs = [
        pl.BlockSpec(memory_space=pltpu.SMEM),
        *[split(count, width) for count in counts],
        *[split(*array.shape[1:]) for array in departure],
    ]
    scratch = [
        pltpu.VMEM((sum(counts), width), F32),
        pltpu.VMEM((len(counts), 256, 128), F32),
        pltpu.VMEM((lev_dev, len(rows_in), tracers, width + 256), F32),
        pltpu.VMEM((lev_dev, 7, len(rows_in), tracers, width), F32),
    ]
    if chemistry is None:
        shapes = [
            (lev_dev, lat_dev, tracers, width), (lev_dev, 3, lat_dev, width),
            (lev_dev, 7, lat_dev, width),
        ]
        out_shape = [jax.ShapeDtypeStruct((segments, *shape), F32) for shape in shapes]
        out_specs = [split(*shape) for shape in shapes]
        scratch.append(pltpu.VMEM((lev_dev, 7, lat_dev, width), F32))
    else:
        regime, production, loss_rate = chemistry
        operands += [regime, production.T, loss_rate.T]
        in_specs += [
            whole(regime.shape), whole(production.shape[::-1]), whole(production.shape[::-1]),
        ]
        out_shape = (
            jax.ShapeDtypeStruct((segments, lev_all, tracers, lat_dev, width), BF16),
            jax.ShapeDtypeStruct((segments, own_rows, width), BF16),
        )
        out_specs = (split(lev_dev, tracers, lat_dev, width), split(own_rows, width))
        scratch += [
            pltpu.VMEM((lat_dev, tracers, width), F32),
            pltpu.VMEM((lat_dev, tracers, width), F32),
            pltpu.VMEM((lev_dev, blocks, tracers * lat_dev, 128), F32),
            pltpu.VMEM((own_rows, width), F32),
        ]
    return pl.pallas_call(
        body,
        out_shape=out_shape,
        grid=(segments // per_step,),
        in_specs=in_specs,
        out_specs=out_specs,
        scratch_shapes=scratch,
        compiler_params=params(),
        cost_estimate=cost(14 if chemistry is None else 6),
        name="advect_own" if chemistry is None else "advect_sides",
    )(*operands)


def fourier_forward(pair_row, quad, received, table, lev_dev, tracers, lat_dev, count):
    pairs = pair_row.shape[1]
    segments, rows, width = received.shape
    step_rows = lev_dev * tracers
    blocks = width // 128

    def body(pair_ref, quad_ref, in_ref, table_hbm, out_ref, table_ref, folded, sem):
        copy = pltpu.make_async_copy(table_hbm, table_ref, sem)
        copy.start()
        turn = mirror()
        zero = jnp.zeros((rows, 128), F32)

        def block(k):
            at = k % blocks * 128
            return in_ref[k // blocks, :, at : at + 128]

        def mirrored(i, end):
            low, high = end // 128 - i - 1, end // 128 - i
            if i == 0:
                return jnp.dot(block(low), turn[:128], preferred_element_type=F32)
            if i == QUARTER // 128:
                return jnp.dot(block(high), turn[128:], preferred_element_type=F32)
            both = jnp.concatenate([block(low), block(high)], axis=1)
            return jnp.dot(both, turn, preferred_element_type=F32)

        for i in range(SPAN // 128):
            inside = i < QUARTER // 128
            one = block(i).astype(F32) if inside else zero
            two = block(NLON // 256 + i).astype(F32) if inside else zero
            one_back, two_back = mirrored(i, NLON // 2), mirrored(i, NLON)
            outer, inner = one + two_back, one_back + two
            outer_less, inner_less = one - two_back, two - one_back
            lanes = slice(i * 128, (i + 1) * 128)
            folded[0, :, lanes] = (outer + inner).astype(BF16)
            folded[1, :, lanes] = (outer_less + inner_less).astype(BF16)
            folded[2, :, lanes] = (outer - inner).astype(BF16)
            folded[3, :, lanes] = (outer_less - inner_less).astype(BF16)
        hits = one_hot(pair_ref[...])
        copy.wait()

        def product(k):
            result = jnp.dot(
                folded[k],
                table_ref[k * SPAN : (k + 1) * SPAN, :],
                preferred_element_type=F32,
            )
            pieces = [
                result[j * step_rows : (j + 1) * step_rows] * quad_ref[j] for j in range(lat_dev)
            ]
            return jnp.concatenate(pieces, axis=0)

        first = lax.broadcasted_iota(jnp.int32, (1, pairs), 1) < HALF
        groups = [None] * (4 * lat_dev * lev_dev)
        for r in range(2):
            by_parity = [product(r), product(2 + r)]
            for s in range(2):
                value = jnp.where(first, by_parity[s], by_parity[1 - s]).astype(BF16)
                value = jnp.dot(value, hits, preferred_element_type=F32)
                for j in range(lat_dev):
                    for l in range(lev_dev):
                        start = (j * lev_dev + l) * tracers
                        groups[((j * 2 + s) * lev_dev + l) * 2 + r] = value[
                            start : start + tracers
                        ]
        turned = jnp.concatenate(groups, axis=0).T
        each = pairs // count
        for d in range(count):
            out_ref[d] = turned[d * each : (d + 1) * each].astype(BF16)

    shape = (count, pairs // count, 4 * rows)
    return pl.pallas_call(
        body,
        out_shape=jax.ShapeDtypeStruct(shape, BF16),
        in_specs=[
            pl.BlockSpec(memory_space=pltpu.VMEM),
            pl.BlockSpec(memory_space=pltpu.SMEM),
            pl.BlockSpec(memory_space=pltpu.VMEM),
            pl.BlockSpec(memory_space=pl.ANY),
        ],
        out_specs=pl.BlockSpec(memory_space=pltpu.VMEM),
        scratch_shapes=[
            pltpu.VMEM(table.shape, BF16),
            pltpu.VMEM((4, rows, SPAN), BF16),
            pltpu.SemaphoreType.DMA,
        ],
        compiler_params=params(),
        cost_estimate=cost(5),
        name="fourier_forward",
    )(pair_row, quad, received, table)


def legendre_forward(own_pairs, received, legendre, lev_dev, tracers):
    count, pair_dev, _ = received[0].shape
    length, lats = legendre.shape[1:]
    lat_dev = lats // count
    widths = [4 * levels * tracers for _, levels in CHUNKS]
    rows = sum(widths)
    groups = row_groups(lev_dev, tracers)
    back = [groups.index(start) * tracers for start in range(0, rows, tracers)]
    group = 8

    def body(pairs, *rest):
        ins, rest = rest[: len(CHUNKS)], rest[len(CHUNKS) :]
        table_hbm, out_ref, turned, tables_ref, sems = rest
        step = pl.program_id(0)

        def copy(k):
            at = pl.ds(k * group, group)
            return pltpu.make_async_copy(table_hbm.at[at], tables_ref.at[at], sems.at[k])

        @pl.when(step == 0)
        def _():
            for k in range(pair_dev // group):
                copy(k).start()
            for s in range(count):
                values = [ref[s].astype(F32) for ref in ins]
                for j in range(lat_dev):
                    piece = [v[:, j * w : (j + 1) * w] for v, w in zip(values, widths)]
                    piece.append(jnp.zeros((pair_dev, 128 - rows), F32))
                    piece = jnp.concatenate(piece, axis=1)
                    turned[pl.ds(s * lat_dev + j, pair_dev, stride=lats), :] = piece

        copy(step).wait()
        for i in range(group):
            pair = step * group + i
            limit = M - pairs[pair]
            keep = lax.broadcasted_iota(jnp.int32, (1, length), 1) < limit
            left = turned[pl.ds(pl.multiple_of(pair * lats, lats), lats), :].T
            left = jnp.concatenate([left[at : at + tracers] for at in back], axis=0)
            both = lax.dot_general(
                left.astype(BF16),
                tables_ref[pair],
                (((1,), (1,)), ((), ())),
                preferred_element_type=F32,
            )
            out_ref[i] = jnp.where(keep, both[: rows // 2], both[rows // 2 :]).astype(BF16)

    return pl.pallas_call(
        body,
        out_shape=jax.ShapeDtypeStruct((pair_dev, rows // 2, length), BF16),
        grid=(pair_dev // group,),
        in_specs=[
            pl.BlockSpec(memory_space=pltpu.SMEM),
            *[pl.BlockSpec(array.shape, lambda g: (0, 0, 0)) for array in received],
            pl.BlockSpec(memory_space=pl.ANY),
        ],
        out_specs=pl.BlockSpec((group, rows // 2, length), lambda g: (g, 0, 0)),
        scratch_shapes=[
            pltpu.VMEM((pair_dev * lats, 128), F32),
            pltpu.VMEM(legendre.shape, BF16),
            pltpu.SemaphoreType.DMA((pair_dev // group,)),
        ],
        compiler_params=params(),
        cost_estimate=cost(13),
        name="legendre_forward",
    )(own_pairs, *received, legendre)


def per_device(
    spectral,
    legendre,
    pair_of_slot,
    quad_weights,
    departure_row,
    departure_column,
    fraction_row,
    fraction_column,
    regime,
    production,
    loss_rate,
):
    pair_dev, lev_dev, _, tracers, length = spectral.shape
    lat_dev, width = departure_row.shape[1:]
    count, segments = lax.axis_size("lat"), lax.axis_size("fld")
    band, segment = lax.axis_index("lat"), lax.axis_index("fld")
    table, sides, table_turned = tables(segments)
    own_pairs = lax.dynamic_slice_in_dim(pair_of_slot, band * pair_dev, pair_dev)
    pair_row = pair_of_slot[None, :]
    exchange = functools.partial(lax.all_to_all, split_axis=0, concat_axis=0, tiled=True)

    packed = spectral.reshape(pair_dev, lev_dev * 2 * tracers, length)
    coeffs = legendre_back(
        own_pairs, packed, legendre.transpose(1, 0, 2), count, lev_dev, tracers
    )
    where = jnp.stack([band * lat_dev, segment * width]).astype(jnp.int32)
    quad = quad_weights * (1.0 / math.sqrt(NLON))
    up = [(i, (i + 1) % count) for i in range(count)]
    down = [(b, a) for a, b in up]
    back, tracers_out = [], None
    for (first, levels), part in zip(CHUNKS, coeffs):
        part = exchange(part, "lat")
        grid = fourier_back(pair_row, part, table, sides, levels, tracers, lat_dev, segments)
        grid = exchange(grid, "fld")
        near = 3 * levels * tracers + 8
        before = lax.ppermute(grid[:, near - 8 : 2 * near - 8], "lat", up)
        after = lax.ppermute(grid[:, :near], "lat", down)
        departure = (departure_row, departure_column, fraction_row, fraction_column)
        departure = [array.reshape(segments, -1, lat_dev, width) for array in departure]
        sums = advect(where, [grid], departure, levels, tracers, lat_dev)
        tracers_out, rows = advect(
            where, [before, after], sums, levels, tracers, lat_dev, (regime, production, loss_rate)
        )
        rows = exchange(rows, "fld")
        part = fourier_forward(pair_row, quad, rows, table_turned, levels, tracers, lat_dev, count)
        back.append(exchange(part, "lat"))
    spectral_out = legendre_forward(own_pairs, back, legendre, lev_dev, tracers)
    tracers_out = tracers_out.reshape(-1, tracers, lat_dev, width)
    return spectral_out.reshape(spectral.shape), tracers_out


def solution(mesh):
    placed = (
        P("lat", "fld", None, None, None),
        P("lat", None, None),
        P(),
        P("lat"),
        P(None, "lat", "fld"),
        P(None, "lat", "fld"),
        P(None, "lat", "fld"),
        P(None, "lat", "fld"),
        P("lat", "fld"),
        P(),
        P(),
    )
    return jax.shard_map(
        per_device,
        mesh=mesh,
        in_specs=placed,
        out_specs=(P("lat", "fld", None, None, None), P(None, None, "lat", "fld")),
        check_vma=False,
    )
```
